256 devices in a mesh: pt: 32 (over z, x), lm: 8 (over y, core).
Axes of the slice: x: 4, y: 4, z: 8, core: 2. Of those that a mesh axis runs over, the one named last changes fastest.
Arguments:
- points: float32 [262144, 256], P('pt'), may hold values from -6 to 6
- landmarks: float32 [8192, 256], P(('lm', 'pt')), may hold values from -6 to 6
- block_vec: float32 [8192, 32], P(('lm', 'pt')), may hold values from -6 to 6
Outputs:
- new_block: float32 [8192, 32], P(('lm', 'pt'))
- projected: float32 [262144, 32], P('pt')
The draws below stay inside these ranges and needn't reach their ends.
All inputs are finite; a program needn't handle non-finite values.
Results may differ from the reference program's by a relative error of at most 0.0056.
Values may be sent and summed in bfloat16 or wider, within the bound.
A program may use at most 128 MiB of HBM per device.

```python
import math
import jax
import jax.numpy as jnp
from jax import lax

D = 256
LANDMARKS = 8192
BLOCK = 32
PT_DEV = 8192
NPTS = 262144
N_PT = 32


topic_count = 16


def shared_direction(key):
    signs = jax.random.bernoulli(key, 0.5, (D,))
    return jnp.where(signs, 1.0, -1.0).astype(jnp.float32) / math.sqrt(D)


def shared_topics(key):
    topic_key = jax.random.fold_in(key, 5)
    signs = jax.random.bernoulli(topic_key, 0.5, (topic_count, D))
    return jnp.where(signs, 1.0, -1.0).astype(jnp.float32)


def drawn_rows(noise, coefs, topics, lower, upper, direction):
    count = noise.shape[0]
    position = jnp.arange(count, dtype=jnp.float32) / count
    along = lower + (upper - lower) * position
    mixed = noise
    weight = jnp.ones((count,), jnp.float32)
    for index in range(topic_count):
        mixed = mixed + coefs[:, index:index + 1] * topics[index][None, :]
        weight = weight + coefs[:, index] * coefs[:, index]
    stretch = along * jnp.sqrt(weight) / jnp.sqrt(1.0 - along * along)
    mixed = mixed + (stretch * math.sqrt(D))[:, None] * direction[None, :]
    return jnp.clip(mixed, -6.0, 6.0)


def draw_points(key, part):
    direction = shared_direction(key)
    topics = shared_topics(key)
    key = jax.random.fold_in(key, 11)
    noise_key = jax.random.fold_in(key, 1)
    coef_key = jax.random.fold_in(key, 2)
    noise = jax.random.truncated_normal(noise_key, -4.0, 4.0, (NPTS, D), jnp.float32)
    coefs = 0.3 * jax.random.truncated_normal(coef_key, -3.0, 3.0, (NPTS, topic_count), jnp.float32)
    return drawn_rows(noise, coefs, topics, 0.2, 0.6, direction)


def draw_landmarks(key, part):
    direction = shared_direction(key)
    topics = shared_topics(key)
    key = jax.random.fold_in(key, 12)
    noise_key = jax.random.fold_in(key, 1)
    coef_key = jax.random.fold_in(key, 2)
    noise = jax.random.truncated_normal(noise_key, -4.0, 4.0, (LANDMARKS, D), jnp.float32)
    coefs = 0.3 * jax.random.truncated_normal(coef_key, -3.0, 3.0, (LANDMARKS, topic_count), jnp.float32)
    return drawn_rows(noise, coefs, topics, 0.2, 0.6, direction)


def steps_of(own_key, extent, split, smallest, high):
    loudness, own = 1.0, jax.random.fold_in(own_key, 6)
    for axis_at, parts in split:
        heights = jnp.exp(jax.random.uniform(jax.random.fold_in(own, axis_at), (parts,), jnp.float32, smallest / len(split), high / len(split)))
        loudness = loudness * jnp.repeat(heights, extent[axis_at] // parts).reshape([-1 if axis == axis_at else 1 for axis in range(len(extent))])
    return loudness


def centred(own_key, shape, deviation, most, pieces=(), held_as=jnp.bfloat16):
    values = jax.random.normal(own_key, shape, jnp.float32) * deviation
    if len(pieces) > 0:
        values = steps_of(own_key, shape, pieces, -0.22, 0.18) * values
    return jnp.clip(values, min=-most, max=most).astype(held_as)


def setup_inputs(seed: int = 0) -> dict:
    seeds = jax.random.split(jax.random.key(seed), 4)
    points = draw_points(jax.random.fold_in(seeds[3], 71), 0)
    landmarks = draw_landmarks(jax.random.fold_in(seeds[3], 71), 0)
    block_vec = centred(seeds[2], (LANDMARKS, BLOCK), 1.0, 6.0, ((0, 256),), jnp.float32)
    return {"points": points, "landmarks": landmarks, "block_vec": block_vec}


def normalize(rows):
    rows = rows.astype(jnp.float32)
    return (rows * lax.rsqrt(lax.optimization_barrier(jnp.sum(rows * rows, axis=1, keepdims=True)) + 1e-06)).astype(jnp.bfloat16)

def reference(points, landmarks, block_vec):
    unit_pts = normalize(points)
    unit_lms = normalize(landmarks)
    blocks = unit_pts.reshape(N_PT, PT_DEV, D)

    def one(rows):
        scores = lax.dot_general(rows, unit_lms, (((1,), (1,)), ((), ())), preferred_element_type=jnp.float32)
        return jnp.exp(16.0 * scores).astype(jnp.bfloat16)
    kernel = lax.map(one, blocks).reshape(NPTS, LANDMARKS)
    row_mean = lax.optimization_barrier(jnp.sum(kernel, axis=1, dtype=jnp.float32)) / LANDMARKS
    col_mean = lax.optimization_barrier(jnp.sum(kernel, axis=0, dtype=jnp.float32)) / NPTS
    scaled = (block_vec * lax.rsqrt(col_mean)[:, None]).astype(jnp.bfloat16)
    row_scale = lax.rsqrt(row_mean)[:, None]
    projected = jnp.dot(kernel, scaled, preferred_element_type=jnp.float32) * row_scale * (1.0 / math.sqrt(LANDMARKS))
    carried = (projected * row_scale).astype(jnp.bfloat16)
    back = lax.dot_general(kernel, carried, (((0,), (0,)), ((), ())), preferred_element_type=jnp.float32)
    new_block = back * lax.rsqrt(col_mean)[:, None] * (1.0 / math.sqrt(NPTS))
    return (new_block, projected)
```

```python
import functools
import math

import jax
import jax.numpy as jnp
from jax import lax
from jax.experimental import pallas as pl
from jax.experimental.pallas import tpu as pltpu
from jax.sharding import PartitionSpec as P

MESH = pl.DeviceIdType.MESH
NX = 4
PAIR = 256
EXP2_SCALE = 16.0 / math.log(2.0)
LAST = (((1,), (1,)), ((), ()))


def unit_rows(rows):
    return (rows * lax.rsqrt(jnp.sum(rows * rows, axis=1, keepdims=True) + 1e-06)).astype(
        jnp.bfloat16
    )


def at(start, size):
    return pl.ds(pl.multiple_of(start, size), size)


def kernel(
    npt, nlm, total_points, total_landmarks,
    points, landmarks, vectors, new_block, projected,
    raw, unit, lms, tile, tile_t, cols_x, cols_z, col_inv, vec_x, vec_z, scaled, rows_all, rows_inv,
    part, part_in, proj, back_out, back_in, back_x,
    raw_sem, lz_s, lz_r, lx_s, lx_r, vx_s, vx_r, vz_s, vz_r, cx_s, cx_r, cz_s, cz_r,
    row_s, row_r, ps_s, ps_r, pg_s, pg_r, bz_s, bz_r, bx_s, bx_r,
):
    count, depth = unit.shape
    own, width = vectors.shape
    nz = npt // NX
    group = NX * own
    chunks = part_in.shape[0]
    chunk = count // chunks
    piece = chunk // nlm
    pt = lax.axis_index("pt")
    lm = lax.axis_index("lm")
    z, x = pt // NX, lax.rem(pt, NX)

    def z_at(step):
        return lax.rem(z + step, nz)

    def x_at(step):
        return lax.rem(x + step, NX)

    def lm_at(step):
        return lax.rem(lm + step, nlm)

    def z_dev(step):
        return (z_at(step) * NX + x, lm)

    def x_dev(step):
        return (z * NX + x_at(step), lm)

    def lm_dev(step):
        return (pt, lm_at(step))

    def remote(src, dst, send, recv, device):
        return pltpu.make_async_remote_copy(
            src_ref=src, dst_ref=dst, send_sem=send, recv_sem=recv,
            device_id=device, device_id_type=MESH,
        )

    sent = []

    def send(*args):
        copy = remote(*args)
        copy.start()
        sent.append(copy)
        return copy

    z_order = [1, nz - 1, 2, nz - 2, 3, nz - 3, 4]
    x_order = [1, 3, 2]
    lm_order = list(range(1, nlm))

    parts = raw_sem.shape[0]
    rows_in = count // parts
    loads = [
        pltpu.make_async_copy(
            points.at[pl.ds(i * rows_in, rows_in), :],
            raw.at[pl.ds(i * rows_in, rows_in), :],
            raw_sem.at[i],
        )
        for i in range(parts)
    ]
    for load in loads:
        load.start()

    barrier = pltpu.get_barrier_semaphore()
    for d in z_order:
        pl.semaphore_signal(barrier, inc=1, device_id=z_dev(d), device_id_type=MESH)
    for e in x_order:
        pl.semaphore_signal(barrier, inc=1, device_id=x_dev(e), device_id_type=MESH)
    for f in lm_order:
        pl.semaphore_signal(barrier, inc=1, device_id=lm_dev(f), device_id_type=MESH)

    lms[at(pt * own, own), :] = unit_rows(landmarks[...])
    lane = lax.broadcasted_iota(jnp.int32, (width, group), 1)
    wide = jnp.concatenate([vectors[...], jnp.zeros((own, group - width), jnp.float32)], axis=1)
    turned = jnp.concatenate([wide] * NX, axis=0).T[:width, :]
    vec_x[x] = jnp.where(lane // own == x, turned, 0.0)

    pl.semaphore_wait(barrier, len(z_order) + len(x_order) + len(lm_order))

    def lm_rows(zz, xx):
        return lms.at[at((zz * NX + xx) * own, own), :]

    mine = lm_rows(z, x)
    for d in z_order:
        send(mine, mine, lz_s.at[d], lz_r.at[d], z_dev(d))
    for e in x_order:
        send(mine, mine, lx_s.at[e], lx_r.at[e], x_dev(e))
    vec_copies = [send(vec_x.at[x], vec_x.at[x], vx_s.at[e], vx_r.at[e], x_dev(e)) for e in x_order]

    for i, load in enumerate(loads):
        load.wait()
        rows = pl.ds(i * rows_in, rows_in)
        unit[rows, :] = unit_rows(raw[rows, :])

    for d in z_order:
        block = lm_rows(z_at(nz - d), x)
        remote(block, block, lz_s.at[d], lz_r.at[d], z_dev(d)).wait_recv()
        for e in x_order:
            send(block, block, lx_s.at[d * NX + e], lx_r.at[d * NX + e], x_dev(e))
    for copy in vec_copies:
        copy.wait_recv()
    vec_z[z] = jnp.sum(vec_x[...], axis=0)
    vec_copies = [send(vec_z.at[z], vec_z.at[z], vz_s.at[d], vz_r.at[d], z_dev(d)) for d in z_order]

    def pair(j, _):
        steps = (lax.rem(nz - j, nz), j + 1)
        groups = [z_at(nz - step) for step in steps]
        for step in steps:
            for e in x_order:
                sem = step * NX + e
                remote(mine, mine, lx_s.at[sem], lx_r.at[sem], x_dev(e)).wait_recv()
        weights = jnp.concatenate([lms[at(g * group, group), :] for g in groups], axis=0)
        scores = lax.dot_general(unit[...], weights, LAST, preferred_element_type=jnp.float32)
        values = jnp.exp2(EXP2_SCALE * scores)
        rounded = values.astype(jnp.bfloat16)
        sums = jnp.sum(values, axis=0, keepdims=True)
        for i, g in enumerate(groups):
            lanes = slice(i * group, (i + 1) * group)
            tile[:, at(g * group, group)] = rounded[:, lanes]
            cols_x[x, pl.ds(g, 1), :] = sums[:, lanes]
        return 0

    lax.fori_loop(0, nz // 2, pair, 0)

    col_copies = [send(cols_x.at[x], cols_x.at[x], cx_s.at[e], cx_r.at[e], x_dev(e)) for e in x_order]

    lanes_per = chunk // group

    def turn(q):
        at_q = pl.ds(q * chunk, chunk)
        tile_t[:, at_q] = tile[at_q, :].T

    def row_sums(q):
        ones = jnp.ones((16, tile_t.shape[0]), jnp.bfloat16)
        sums = jnp.dot(
            ones, tile_t[:, pl.ds(q * chunk, chunk)], preferred_element_type=jnp.float32
        )
        for i in range(lanes_per):
            rows_all[lm, q * lanes_per + i : q * lanes_per + i + 1, :] = sums[
                0:1, i * group : (i + 1) * group
            ]

    turn(0)
    turn(1)
    for copy in col_copies:
        copy.wait_recv()
    cols_z[z] = jnp.sum(cols_x[...], axis=0)
    col_copies = [send(cols_z.at[z], cols_z.at[z], cz_s.at[d], cz_r.at[d], z_dev(d)) for d in z_order]
    for q in range(2, chunks):
        turn(q)
    for q in range(chunks):
        row_sums(q)
    row_copies = [
        send(rows_all.at[lm], rows_all.at[lm], row_s.at[f], row_r.at[f], lm_dev(f)) for f in lm_order
    ]
    for copy in vec_copies:
        copy.wait_recv()
    for copy in col_copies:
        copy.wait_recv()
    col_scale = lax.rsqrt(jnp.sum(cols_z[...], axis=0) * (1.0 / total_points))
    for g in range(nz):
        scaled[:, g * group : (g + 1) * group] = (vec_z[g] * col_scale[g : g + 1, :]).astype(
            jnp.bfloat16
        )
    col_inv[...] = col_scale

    for q in range(chunks):
        at_q = pl.ds(q * chunk, chunk)
        part[:, at_q] = jnp.dot(
            scaled[...], tile_t[:, at_q], preferred_element_type=jnp.float32
        ).astype(jnp.bfloat16)
        for f in lm_order:
            k = q * nlm + f
            send(
                part.at[:, at(q * chunk + lm_at(f) * piece, piece)], part_in.at[q, lm],
                ps_s.at[k], ps_r.at[k], lm_dev(f),
            )
    for copy in row_copies:
        copy.wait_recv()
    rows_inv[...] = lax.rsqrt(jnp.sum(rows_all[...], axis=0) * (1.0 / total_landmarks))
    for q in range(chunks):
        mine_q = at(q * chunk + lm * piece, piece)
        total = part[:, mine_q].astype(jnp.float32)
        for f in lm_order:
            k = q * nlm + f
            remote(
                part.at[:, pl.ds(0, piece)], part_in.at[q, 0], ps_s.at[k], ps_r.at[k], lm_dev(f)
            ).wait_recv()
        for f in lm_order:
            total = total + part_in[q, lm_at(f)].astype(jnp.float32)
        per = piece // group
        first = q * lanes_per + lm * per
        scale = jnp.concatenate([rows_inv[pl.ds(first + i, 1), :] for i in range(per)], axis=1)
        proj[:, mine_q] = (total * scale * (1.0 / math.sqrt(total_landmarks))).astype(jnp.bfloat16)
        for f in lm_order:
            k = q * nlm + f
            send(proj.at[:, mine_q], proj.at[:, mine_q], pg_s.at[k], pg_r.at[k], lm_dev(f))

    back = jnp.zeros((width, tile.shape[1]), jnp.float32)
    for q in range(chunks):
        at_q = pl.ds(q * chunk, chunk)
        for f in lm_order:
            k = q * nlm + f
            some = proj.at[:, pl.ds(0, piece)]
            remote(some, some, pg_s.at[k], pg_r.at[k], lm_dev(f)).wait_recv()
        values = proj[:, at_q].astype(jnp.float32)
        projected[:, at_q] = values
        scale = jnp.concatenate(
            [rows_inv[q * lanes_per + i : q * lanes_per + i + 1, :] for i in range(lanes_per)], axis=1
        )
        carried = (values * scale).astype(jnp.bfloat16)
        back = back + jnp.dot(carried, tile[at_q, :], preferred_element_type=jnp.float32)

    for g in range(nz):
        back_out[g] = back[:, g * group : (g + 1) * group].astype(jnp.bfloat16)
    copies = [
        send(back_out.at[z_at(d)], back_in.at[z], bz_s.at[d], bz_r.at[d], z_dev(d)) for d in z_order
    ]
    for copy in copies:
        copy.wait_recv()
    total = back_out[z].astype(jnp.float32)
    for d in z_order:
        total = total + back_in[z_at(nz - d)].astype(jnp.float32)
    back_x[x] = total
    copies = [send(back_x.at[x], back_x.at[x], bx_s.at[e], bx_r.at[e], x_dev(e)) for e in x_order]
    for copy in copies:
        copy.wait_recv()
    total = jnp.sum(back_x[...], axis=0) * (
        col_inv[pl.ds(z, 1), :] * (1.0 / math.sqrt(total_points))
    )
    wide = jnp.concatenate([total, jnp.zeros((group - width, group), jnp.float32)], axis=0)
    turned = wide.T
    chosen = turned[:own, :]
    for i in range(1, NX):
        chosen = jnp.where(x == i, turned[i * own : (i + 1) * own, :], chosen)
    new_block[...] = chosen[:, :width]

    for copy in sent:
        copy.wait_send()


def on_device(points, landmarks, block_vec):
    npt, nlm = lax.axis_size("pt"), lax.axis_size("lm")
    count, depth = points.shape
    own, width = block_vec.shape
    nz = npt // NX
    held = npt * own
    group = NX * own
    chunks = 4
    piece = count // chunks // nlm
    f32, bf16 = jnp.float32, jnp.bfloat16
    dma = lambda n: pltpu.SemaphoreType.DMA((n,))
    vmem = pl.BlockSpec(memory_space=pltpu.VMEM)
    new_block, projected = pl.pallas_call(
        functools.partial(kernel, npt, nlm, count * npt, held * nlm),
        out_shape=(
            jax.ShapeDtypeStruct((own, width), f32),
            jax.ShapeDtypeStruct((width, count), f32),
        ),
        in_specs=[pl.BlockSpec(memory_space=pl.ANY), vmem, vmem],
        out_specs=(vmem, vmem),
        scratch_shapes=[
            pltpu.VMEM((count, depth), f32),
            pltpu.VMEM((count, depth), bf16),
            pltpu.VMEM((held, depth), bf16),
            pltpu.VMEM((count, held), bf16),
            pltpu.VMEM((held, count), bf16),
            pltpu.VMEM((NX, nz, group), f32),
            pltpu.VMEM((nz, nz, group), f32),
            pltpu.VMEM((nz, group), f32),
            pltpu.VMEM((NX, width, group), f32),
            pltpu.VMEM((nz, width, group), f32),
            pltpu.VMEM((width, held), bf16),
            pltpu.VMEM((nlm, count // group, group), f32),
            pltpu.VMEM((count // group, group), f32),
            pltpu.VMEM((width, count), bf16),
            pltpu.VMEM((chunks, nlm, width, piece), bf16),
            pltpu.VMEM((width, count), bf16),
            pltpu.VMEM((nz, width, group), bf16),
            pltpu.VMEM((nz, width, group), bf16),
            pltpu.VMEM((NX, width, group), f32),
            dma(8),
            dma(nz), dma(nz),
            dma(npt), dma(npt),
            dma(NX), dma(NX),
            dma(nz), dma(nz),
            dma(NX), dma(NX),
            dma(nz), dma(nz),
            dma(nlm), dma(nlm),
            dma(chunks * nlm), dma(chunks * nlm),
            dma(chunks * nlm), dma(chunks * nlm),
            dma(nz), dma(nz),
            dma(NX), dma(NX),
        ],
        compiler_params=pltpu.CompilerParams(
            collective_id=0, has_side_effects=True, vmem_limit_bytes=60 * 2**20
        ),
    )(points, landmarks, block_vec)
    return new_block, projected.T


def solution(mesh):
    return jax.shard_map(
        on_device,
        mesh=mesh,
        in_specs=(P("pt", None), P(("lm", "pt"), None), P(("lm", "pt"), None)),
        out_specs=(P(("lm", "pt"), None), P("pt", None)),
        check_vma=False,
    )
```

```python
import functools
import math

import jax
import jax.numpy as jnp
from jax import lax
from jax.experimental import pallas as pl
from jax.experimental.pallas import tpu as pltpu
from jax.sharding import PartitionSpec as P

MESH = pl.DeviceIdType.MESH
NX = 4
PAIR = 256
EXP2_SCALE = 16.0 / math.log(2.0)
LAST = (((1,), (1,)), ((), ()))


def unit_rows(rows):
    return (rows * lax.rsqrt(jnp.sum(rows * rows, axis=1, keepdims=True) + 1e-06)).astype(
        jnp.bfloat16
    )


def at(start, size):
    return pl.ds(pl.multiple_of(start, size), size)


def kernel(
    npt, nlm, total_points, total_landmarks,
    points, landmarks_in, vectors_in, new_block, projected,
    raw, landmarks, vectors, unit, lms, tile, tile_t, cols, col_inv, vec_x, vec_z, scaled, rows_part, rows_got, rows_inv,
    part, part_in, proj, proj_out, back_out, back_in,
    raw_sem, own_sem, out_sem, lz_s, lz_r, lx_s, lx_r, vx_s, vx_r, vz_s, vz_r, c_s, c_r,
    row_s, row_r, ps_s, ps_r, pg_s, pg_r, b_s, b_r,
):
    count, depth = unit.shape
    own, width = vectors.shape
    nz = npt // NX
    group = NX * own
    chunks = part_in.shape[0]
    chunk = count // chunks
    piece = chunk // nlm
    pt = lax.axis_index("pt")
    lm = lax.axis_index("lm")
    z, x = pt // NX, lax.rem(pt, NX)

    def z_at(step):
        return lax.rem(z + step, nz)

    def x_at(step):
        return lax.rem(x + step, NX)

    def lm_at(step):
        return lax.rem(lm + step, nlm)

    def z_dev(step):
        return (z_at(step) * NX + x, lm)

    def x_dev(step):
        return (z * NX + x_at(step), lm)

    def pt_at(step):
        return lax.rem(pt + step, npt)

    def pt_dev(step):
        return (pt_at(step), lm)

    def lm_dev(step):
        return (pt, lm_at(step))

    def remote(src, dst, send, recv, device):
        return pltpu.make_async_remote_copy(
            src_ref=src, dst_ref=dst, send_sem=send, recv_sem=recv,
            device_id=device, device_id_type=MESH,
        )

    sent = []

    def send(*args):
        copy = remote(*args)
        copy.start()
        sent.append(copy)
        return copy

    def drain():
        for copy in sent:
            copy.wait_send()
        sent.clear()

    near, far = [1, nz - 1], [2, nz - 2, 3, nz - 3, 4]
    z_order = far[::-1] + near
    x_order = [1, 3, 2]
    lm_order = list(range(1, nlm))
    pt_order = sorted(range(1, npt), key=lambda step: -min(step, npt - step))

    own_loads = [
        pltpu.make_async_copy(landmarks_in, landmarks, own_sem.at[0]),
        pltpu.make_async_copy(vectors_in, vectors, own_sem.at[1]),
    ]
    for load in own_loads:
        load.start()

    parts = raw_sem.shape[0]
    rows_in = count // parts

    def load(i):
        rows = at(i * rows_in, rows_in)
        return pltpu.make_async_copy(points.at[rows, :], raw.at[rows, :], raw_sem.at[i])

    for i in range(parts):
        load(i).start()

    barrier = pltpu.get_barrier_semaphore()
    for step in pt_order:
        pl.semaphore_signal(barrier, inc=1, device_id=pt_dev(step), device_id_type=MESH)
    for f in lm_order:
        pl.semaphore_signal(barrier, inc=1, device_id=lm_dev(f), device_id_type=MESH)

    own_loads[0].wait()
    lms[at(pt * own, own), :] = unit_rows(landmarks[...])
    pl.semaphore_wait(barrier, len(pt_order) + len(lm_order))

    def lm_rows(zz, xx):
        return lms.at[at((zz * NX + xx) * own, own), :]

    mine = lm_rows(z, x)
    for d in z_order:
        send(mine, mine, lz_s.at[d], lz_r.at[d], z_dev(d))
    for d in [0] + near:
        for e in x_order:
            device = (z_at(d) * NX + x_at(e), lm)
            send(mine, mine, lx_s.at[d * NX + e], lx_r.at[d * NX + e], device)

    own_loads[1].wait()
    lane = lax.broadcasted_iota(jnp.int32, (width, group), 1)
    wide = jnp.concatenate([vectors[...], jnp.zeros((own, group - width), jnp.float32)], axis=1)
    turned = jnp.concatenate([wide] * NX, axis=0).T[:width, :]
    vec_x[x] = jnp.where(lane // own == x, turned, 0.0)

    vec_copies = [send(vec_x.at[x], vec_x.at[x], vx_s.at[e], vx_r.at[e], x_dev(e)) for e in x_order]

    def unit_part(i, _):
        load(i).wait()
        rows = at(i * rows_in, rows_in)
        unit[rows, :] = unit_rows(raw[rows, :])
        return 0

    def go_on(d):
        block = lm_rows(z_at(nz - d), x)
        remote(block, block, lz_s.at[d], lz_r.at[d], z_dev(d)).wait_recv()
        for e in x_order:
            send(block, block, lx_s.at[d * NX + e], lx_r.at[d * NX + e], x_dev(e))

    lax.fori_loop(0, parts - 2, unit_part, 0)
    go_on(2)
    go_on(nz - 2)
    lax.fori_loop(parts - 2, parts, unit_part, 0)
    go_on(3)
    go_on(nz - 3)
    go_on(4)
    for d in near:
        block = lm_rows(z_at(nz - d), x)
        remote(block, block, lz_s.at[d], lz_r.at[d], z_dev(d)).wait_recv()
    for copy in vec_copies:
        copy.wait_recv()
    vec_z[z] = jnp.sum(vec_x[...], axis=0)
    vec_copies = [send(vec_z.at[z], vec_z.at[z], vz_s.at[d], vz_r.at[d], z_dev(d)) for d in z_order]

    def pair(j, _):
        steps = (lax.rem(nz - j, nz), j + 1)
        groups = [z_at(nz - step) for step in steps]
        for step in steps:
            for e in x_order:
                sem = step * NX + e
                remote(mine, mine, lx_s.at[sem], lx_r.at[sem], x_dev(e)).wait_recv()
        weights = jnp.concatenate([lms[at(g * group, group), :] for g in groups], axis=0)
        scores = lax.dot_general(unit[...], weights, LAST, preferred_element_type=jnp.float32)
        values = jnp.exp2(EXP2_SCALE * scores)
        rounded = values.astype(jnp.bfloat16)
        sums = jnp.sum(values, axis=0, keepdims=True)
        for i, g in enumerate(groups):
            lanes = slice(i * group, (i + 1) * group)
            tile[:, at(g * group, group)] = rounded[:, lanes]
            cols[pt, pl.ds(g, 1), :] = sums[:, lanes]
        return 0

    lax.fori_loop(0, nz // 2, pair, 0)

    col_copies = [
        send(cols.at[pt], cols.at[pt], c_s.at[step], c_r.at[step], pt_dev(step)) for step in pt_order
    ]

    lanes_per = chunk // group
    ones = jnp.ones((16, tile.shape[1]), jnp.bfloat16)

    def turn(q, _):
        at_q = at(q * chunk, chunk)
        block = tile[at_q, :]
        tile_t[:, at_q] = block.T
        sums = lax.dot_general(ones, block, LAST, preferred_element_type=jnp.float32)
        for i in range(lanes_per):
            rows_part[pl.ds(q * lanes_per + i, 1), :] = sums[0:1, i * group : (i + 1) * group]
        return 0

    lax.fori_loop(0, chunks, turn, 0)
    row_rows = rows_part.shape[0] // nlm

    def rows_of(owner):
        return at(owner * row_rows, row_rows)

    row_copies = [
        send(rows_part.at[rows_of(lm_at(f)), :], rows_got.at[lm], row_s.at[f], row_r.at[f], lm_dev(f))
        for f in lm_order
    ]
    for copy in vec_copies:
        copy.wait_recv()
    for copy in col_copies:
        copy.wait_recv()
    col_scale = lax.rsqrt(jnp.sum(cols[...], axis=0) * (1.0 / total_points))
    for g in range(nz):
        scaled[:, g * group : (g + 1) * group] = (vec_z[g] * col_scale[g : g + 1, :]).astype(
            jnp.bfloat16
        )
    col_inv[...] = col_scale

    for q in range(chunks):
        at_q = pl.ds(q * chunk, chunk)
        part[:, at_q] = jnp.dot(
            scaled[...], tile_t[:, at_q], preferred_element_type=jnp.float32
        ).astype(jnp.bfloat16)
        for f in lm_order:
            k = q * nlm + f
            send(
                part.at[:, at(q * chunk + lm_at(f) * piece, piece)], part_in.at[q, lm],
                ps_s.at[k], ps_r.at[k], lm_dev(f),
            )
    for copy in row_copies:
        copy.wait_recv()
    total = rows_part[rows_of(lm), :]
    for f in lm_order:
        total = total + rows_got[lm_at(f)]
    rows_inv[rows_of(lm), :] = lax.rsqrt(total * (1.0 / total_landmarks))
    mine_rows = rows_inv.at[rows_of(lm), :]
    row_copies = [
        send(mine_rows, mine_rows, row_s.at[nlm + f], row_r.at[nlm + f], lm_dev(f)) for f in lm_order
    ]
    for q in range(chunks):
        mine_q = at(q * chunk + lm * piece, piece)
        total = part[:, mine_q].astype(jnp.float32)
        for f in lm_order:
            k = q * nlm + f
            remote(
                part.at[:, pl.ds(0, piece)], part_in.at[q, 0], ps_s.at[k], ps_r.at[k], lm_dev(f)
            ).wait_recv()
        for f in lm_order:
            total = total + part_in[q, lm_at(f)].astype(jnp.float32)
        proj[:, mine_q] = total.astype(jnp.bfloat16)
        for f in lm_order:
            k = q * nlm + f
            send(proj.at[:, mine_q], proj.at[:, mine_q], pg_s.at[k], pg_r.at[k], lm_dev(f))

    outs = [
        pltpu.make_async_copy(
            proj_out.at[:, pl.ds(q * chunk, chunk)],
            projected.at[:, pl.ds(q * chunk, chunk)],
            out_sem.at[q],
        )
        for q in range(chunks)
    ]
    for copy in row_copies:
        copy.wait_recv()
    back = jnp.zeros((width, tile.shape[1]), jnp.float32)
    for q in range(chunks):
        at_q = pl.ds(q * chunk, chunk)
        for f in lm_order:
            k = q * nlm + f
            some = proj.at[:, pl.ds(0, piece)]
            remote(some, some, pg_s.at[k], pg_r.at[k], lm_dev(f)).wait_recv()
        scale = jnp.concatenate(
            [rows_inv[q * lanes_per + i : q * lanes_per + i + 1, :] for i in range(lanes_per)], axis=1
        )
        values = proj[:, at_q].astype(jnp.float32) * scale * (1.0 / math.sqrt(total_landmarks))
        proj_out[:, at_q] = values.astype(jnp.bfloat16)
        outs[q].start()
        carried = (values * scale).astype(jnp.bfloat16)
        back = back + jnp.dot(carried, tile[at_q, :], preferred_element_type=jnp.float32)

    bands = width // 8
    lane = lax.broadcasted_iota(jnp.int32, (8, group), 1) // own
    for g in range(nz):
        piece_g = back[:, g * group : (g + 1) * group] * (
            col_inv[g : g + 1, :] * (1.0 / math.sqrt(total_points))
        )
        for i in range(NX):
            packed = jnp.zeros((8, group), jnp.float32)
            for k in range(bands):
                band = piece_g[k * 8 : (k + 1) * 8, :]
                if k != i:
                    band = pltpu.roll(band, (k - i) % bands * own, 1)
                packed = jnp.where(lane == k, band, packed)
            back_out[g * NX + i] = packed
    copies = [
        send(back_out.at[pt_at(step)], back_in.at[pt], b_s.at[step], b_r.at[step], pt_dev(step))
        for step in pt_order
    ]
    back_in[pt] = back_out[pt]
    del sent[-len(copies) :]
    drain()
    for out in outs:
        out.wait()
    for copy in copies:
        copy.wait_recv()
    total = jnp.sum(back_in[...], axis=0)
    bands_in = [total] + [pltpu.roll(total, group - k * own, 1) for k in range(1, bands)]
    square = jnp.concatenate(bands_in + [jnp.zeros((group - width, group), jnp.float32)], axis=0)
    new_block[...] = square.T[:own, :width]
    for copy in copies:
        copy.wait_send()


def widen(block, rounded, new_block, projected, block_in, rounded_in, wide, in_sem, out_sem):
    chunks = out_sem.shape[0]
    chunk = rounded.shape[1] // chunks
    lanes = [pl.ds(q * chunk, chunk) for q in range(chunks)]
    copy_in = [
        pltpu.make_async_copy(rounded.at[:, at_q], rounded_in.at[:, at_q], in_sem.at[q])
        for q, at_q in enumerate(lanes)
    ] + [pltpu.make_async_copy(block, block_in, in_sem.at[chunks])]
    copy_out = [
        pltpu.make_async_copy(wide.at[:, at_q], projected.at[:, at_q], out_sem.at[q])
        for q, at_q in enumerate(lanes)
    ]
    for copy in copy_in:
        copy.start()
    for q, at_q in enumerate(lanes):
        copy_in[q].wait()
        wide[:, at_q] = rounded_in[:, at_q].astype(jnp.float32)
        copy_out[q].start()
    copy_in[chunks].wait()
    new_block[...] = block_in[...]
    for copy in copy_out:
        copy.wait()


def on_device(points, landmarks, block_vec):
    npt, nlm = lax.axis_size("pt"), lax.axis_size("lm")
    count, depth = points.shape
    own, width = block_vec.shape
    nz = npt // NX
    held = npt * own
    group = NX * own
    chunks = 4
    piece = count // chunks // nlm
    f32, bf16 = jnp.float32, jnp.bfloat16
    dma = lambda n: pltpu.SemaphoreType.DMA((n,))
    vmem = pl.BlockSpec(memory_space=pltpu.VMEM)
    block, rounded = pl.pallas_call(
        functools.partial(kernel, npt, nlm, count * npt, held * nlm),
        out_shape=(
            jax.ShapeDtypeStruct((own, width), f32),
            jax.ShapeDtypeStruct((width, count), bf16),
        ),
        in_specs=[pl.BlockSpec(memory_space=pl.ANY)] * 3,
        out_specs=(vmem, pl.BlockSpec(memory_space=pl.ANY)),
        scratch_shapes=[
            pltpu.VMEM((count, depth), f32),
            pltpu.VMEM((own, depth), f32),
            pltpu.VMEM((own, width), f32),
            pltpu.VMEM((count, depth), bf16),
            pltpu.VMEM((held, depth), bf16),
            pltpu.VMEM((count, held), bf16),
            pltpu.VMEM((held, count), bf16),
            pltpu.VMEM((npt, nz, group), f32),
            pltpu.VMEM((nz, group), f32),
            pltpu.VMEM((NX, width, group), f32),
            pltpu.VMEM((nz, width, group), f32),
            pltpu.VMEM((width, held), bf16),
            pltpu.VMEM((count // group, group), f32),
            pltpu.VMEM((nlm, count // group // nlm, group), f32),
            pltpu.VMEM((count // group, group), f32),
            pltpu.VMEM((width, count), bf16),
            pltpu.VMEM((chunks, nlm, width, piece), bf16),
            pltpu.VMEM((width, count), bf16),
            pltpu.VMEM((width, count), bf16),
            pltpu.VMEM((npt, 8, group), f32),
            pltpu.VMEM((npt, 8, group), f32),
            dma(8), dma(2), dma(chunks),
            dma(nz), dma(nz),
            dma(npt), dma(npt),
            dma(NX), dma(NX),
            dma(nz), dma(nz),
            dma(npt), dma(npt),
            dma(2 * nlm), dma(2 * nlm),
            dma(chunks * nlm), dma(chunks * nlm),
            dma(chunks * nlm), dma(chunks * nlm),
            dma(npt), dma(npt),
        ],
        compiler_params=pltpu.CompilerParams(
            collective_id=0, has_side_effects=True, vmem_limit_bytes=60 * 2**20
        ),
    )(points, landmarks, block_vec)
    new_block, projected = pl.pallas_call(
        widen,
        out_shape=(
            jax.ShapeDtypeStruct((own, width), f32),
            jax.ShapeDtypeStruct((width, count), f32),
        ),
        in_specs=[pl.BlockSpec(memory_space=pltpu.HBM)] * 2,
        out_specs=(vmem, pl.BlockSpec(memory_space=pltpu.HBM)),
        scratch_shapes=[
            pltpu.VMEM((own, width), f32),
            pltpu.VMEM((width, count), bf16),
            pltpu.VMEM((width, count), f32),
            dma(chunks + 1),
            dma(chunks),
        ],
        compiler_params=pltpu.CompilerParams(vmem_limit_bytes=60 * 2**20),
    )(block, rounded)
    return new_block, projected.T


def solution(mesh):
    return jax.shard_map(
        on_device,
        mesh=mesh,
        in_specs=(P("pt", None), P(("lm", "pt"), None), P(("lm", "pt"), None)),
        out_specs=(P(("lm", "pt"), None), P("pt", None)),
        check_vma=False,
    )
```
